32 devices in a mesh: seq: 8 (over z, y), tile: 4 (over x, core).
Axes of the slice: x: 2, y: 2, z: 4, core: 2. Of those that a mesh axis runs over, the one named last changes fastest.
Arguments:
- queries: bfloat16 [4096, 2048], P(('seq', 'tile')), may hold values from -4.5 to 4.5
- keys: bfloat16 [4096, 2048], P(('seq', 'tile')), may hold values from -4.5 to 4.5
- values: bfloat16 [4096, 2048], P(('seq', 'tile')), may hold values from -6 to 6
- mod_shift: float32 [2048], replicated, may hold values from -4 to 4
- mod_scale: float32 [2048], replicated, may hold values from -2 to 2
- final_weight: float32 [2048, 64], replicated, may hold values from -0.125 to 0.125
- final_bias: float32 [64], replicated, may hold values from -3 to 3
- tile_widths: int32 [4], replicated, may hold values from 1 to 24, 64 in all
- conv_in_weight: bfloat16 [432, 512], replicated, may hold values from -0.3125 to 0.3125
- conv_in_bias: float32 [512], replicated, may hold values from -3 to 3
- conv_up_weight: bfloat16 [9, 512, 256], replicated, may hold values from -0.09375 to 0.09375
- conv_up_bias: float32 [256], replicated, may hold values from -3 to 3
Outputs:
- pixels: bfloat16 [8, 64, 128, 256], P('seq', None, 'tile')
The draws below stay inside these ranges and needn't reach their ends.
Inputs may be any that keep to these rules, and one draw needn't show every extreme that they name: `tile_widths`: tile widths sum to 64; the widest is exactly 24.
All inputs are finite; a program needn't handle non-finite values.
Results may differ from the reference program's by a relative error of at most 0.011.
Values may be sent and summed in bfloat16 or wider, within the bound.
A program may use at most 128 MiB of HBM per device.

```python
import math
import jax
import jax.numpy as jnp
import numpy as np
from jax import lax

HEADS = 16
HEAD_DIM = 128
LAT_CH = 16
CH_IN = 512
CH_OUT = 256
PR = 16
PC = 32
OV = 2
FEAT = 2048
TOKENS = 4096
FRAMES = 8
WMOST = 24
TW = 28
N_TILE = 4


def draw_queries(key, part):
    key = jax.random.fold_in(key, 11)
    base = jnp.clip(jax.random.normal(key, (TOKENS, FEAT)), -4.5, 4.5)
    return base.astype(jnp.bfloat16)


def draw_keys(key, part):
    key = jax.random.fold_in(key, 12)
    base = jnp.clip(jax.random.normal(key, (TOKENS, FEAT)), -4.5, 4.5)
    return base.astype(jnp.bfloat16)


def level_of(own_key, dims, cuts, smallest, top_value):
    def one(axis_at, shards_of):
        steps = jax.random.uniform(jax.random.fold_in(jax.random.fold_in(own_key, 6), axis_at), (shards_of,), jnp.float32, smallest / len(cuts), top_value / len(cuts))
        return jnp.repeat(jnp.exp(steps), dims[axis_at] // shards_of).reshape((-1,) + (1,) * (len(dims) - axis_at - 1))

    factor_of = one(*cuts[0])
    for cut in cuts[1:]:
        factor_of = factor_of * one(*cut)
    return factor_of


def profile(amount, total, bound, lean):
    loads = [(1 << 20) // math.isqrt(standing ** lean) + 1 for standing in range(2, amount + 1)]
    spare, counts = total - bound - (amount - 1), [1] * (amount - 1)
    while spare > 0:
        candidates = [i for i in range(amount - 1) if counts[i] < bound]
        pool, left = sum([loads[i] for i in candidates]), spare
        for i in candidates:
            addition = min(bound - counts[i], max(1, left * loads[i] // pool), spare)
            counts[i] = counts[i] + addition
            spare = spare - addition
    return np.array([bound] + counts)


def uneven(own_key, amount, total, limit, skew):
    if amount == 2:
        one = jax.random.randint(own_key, (), max(1, total - limit), min(limit, total - 1) + 1)
        return jnp.stack([one, total - one])
    tallies = jnp.asarray(profile(amount, total, limit, skew), jnp.int32)
    twos = (amount - 1) // 2
    giver, receiver = tallies[1:1 + 2 * twos:2], tallies[2:2 + 2 * twos:2]
    margin = jnp.minimum(giver - 1, limit - receiver)
    passed = jax.random.randint(jax.random.fold_in(own_key, 1), (twos,), 0, 1 << 20) % (margin + 1)
    tallies = tallies.at[1:1 + 2 * twos:2].set(giver - passed).at[2:2 + 2 * twos:2].set(receiver + passed)
    return tallies[jax.random.permutation(jax.random.fold_in(own_key, 2), amount)]


def normal_values(key, dims, spread, bound, split=(), kind=jnp.bfloat16):
    values = jax.random.normal(key, dims, jnp.float32) * spread
    if len(split) > 0:
        values = level_of(key, dims, split, -0.22, 0.18) * values
    return jnp.clip(values, min=-bound, max=bound).astype(kind)


def setup_inputs(seed: int = 0) -> dict:
    splits = jax.random.split(jax.random.key(seed), 13)
    return {
        "queries": draw_queries(jax.random.fold_in(splits[12], 71), 0),
        "keys": draw_keys(jax.random.fold_in(splits[12], 71), 0),
        "values": normal_values(splits[2], (TOKENS, FEAT), 1.0, 6.0, ((0, 32),)),
        "mod_shift": normal_values(splits[3], (FEAT,), 1.0, 4.0, (), jnp.float32),
        "mod_scale": normal_values(splits[4], (FEAT,), 0.5, 2.0, (), jnp.float32),
        "final_weight": normal_values(splits[5], (FEAT, 4 * LAT_CH), FEAT ** -0.5, 0.125, (), jnp.float32),
        "final_bias": normal_values(splits[6], (4 * LAT_CH,), 0.5, 3.0, (), jnp.float32),
        "tile_widths": uneven(splits[7], N_TILE, 2 * PC, WMOST, 1).astype(jnp.int32),
        "conv_in_weight": normal_values(splits[8], (27 * LAT_CH, CH_IN), (27 * LAT_CH) ** -0.5, 0.3125),
        "conv_in_bias": normal_values(splits[9], (CH_IN,), 0.5, 3.0, (), jnp.float32),
        "conv_up_weight": normal_values(splits[10], (9, CH_IN, CH_OUT), (9 * CH_IN) ** -0.5, 0.09375),
        "conv_up_bias": normal_values(splits[11], (CH_OUT,), 0.5, 3.0, (), jnp.float32),
    }


def ramp(pos, begin, span):
    dist = jnp.minimum(pos - begin, begin + span - 1 - pos) + 1
    return jnp.clip(dist, 0, 4 * OV).astype(jnp.float32)

def up_block(extended, keep, w_in, b_in, w_up, b_up):
    frames = extended.shape[0] - 2
    rows = extended.shape[1]
    cols = extended.shape[2]
    padded = jnp.pad(extended, ((0, 0), (1, 1), (1, 1), (0, 0)))
    taps = [padded[kt:kt + frames, ky:ky + rows, kx:kx + cols] for kt in range(3) for ky in range(3) for kx in range(3)]
    stacked = jnp.concatenate(taps, axis=-1)
    hidden = jnp.dot(stacked.reshape(-1, stacked.shape[-1]), w_in, preferred_element_type=jnp.float32) + b_in
    hidden = jax.nn.silu(hidden).reshape(frames, rows, cols, -1) * keep[None, None, :, None]
    hidden = hidden.astype(jnp.bfloat16)
    grown = jnp.repeat(jnp.repeat(hidden, 2, axis=1), 2, axis=2)
    grown = jnp.pad(grown, ((0, 0), (1, 1), (1, 1), (0, 0)))
    total = jnp.zeros((frames * 2 * rows * 2 * cols, w_up.shape[2]), jnp.float32)
    for ky in range(3):
        for kx in range(3):
            window_part = grown[:, ky:ky + 2 * rows, kx:kx + 2 * cols].reshape(-1, grown.shape[-1])
            total = total + jnp.dot(window_part, w_up[ky * 3 + kx], preferred_element_type=jnp.float32)
    total = total + b_up
    return total.reshape(frames, 2 * rows, 2 * cols, -1).astype(jnp.bfloat16)

def final_norm(attended, mod_shift, mod_scale, final_weight, final_bias):
    feats = attended.astype(jnp.float32)
    mean_val = lax.optimization_barrier(jnp.mean(feats, axis=1, keepdims=True))
    var_val = lax.optimization_barrier(jnp.mean((feats - mean_val) ** 2, axis=1, keepdims=True))
    normed = (feats - mean_val) / jnp.sqrt(var_val + 1e-06) * (1.0 + mod_scale) + mod_shift
    patches = jnp.dot(normed, final_weight, precision=lax.Precision.HIGHEST) + final_bias
    return patches.astype(jnp.bfloat16)

def reference(queries, keys, values, mod_shift, mod_scale, final_weight, final_bias, tile_widths, conv_in_weight, conv_in_bias, conv_up_weight, conv_up_bias):
    scale = HEAD_DIM ** (-0.5)
    block = math.gcd(TOKENS, 1024)
    q_heads = queries.reshape(TOKENS, HEADS, HEAD_DIM).transpose(1, 0, 2)
    k_heads = keys.reshape(TOKENS, HEADS, HEAD_DIM).transpose(1, 0, 2)
    v_heads = values.reshape(TOKENS, HEADS, HEAD_DIM).transpose(1, 0, 2)

    def one_head(args):
        q_one, k_one, v_one = args

        def one_block(q_blk):
            scores = jnp.dot(q_blk, k_one.T, preferred_element_type=jnp.float32) * scale
            top = lax.optimization_barrier(jnp.max(scores, axis=1, keepdims=True))
            probs = jnp.exp(scores - top)
            denom = lax.optimization_barrier(jnp.sum(probs, axis=1, keepdims=True))
            mixed = jnp.dot(probs.astype(jnp.bfloat16), v_one, preferred_element_type=jnp.float32)
            return (mixed / denom).astype(jnp.bfloat16)
        return lax.map(one_block, q_one.reshape(-1, block, HEAD_DIM)).reshape(TOKENS, HEAD_DIM)
    attended = lax.map(one_head, (q_heads, k_heads, v_heads))
    attended = attended.transpose(1, 0, 2).reshape(TOKENS, FEAT)
    patches = final_norm(attended, mod_shift, mod_scale, final_weight, final_bias)
    latent = patches.reshape(FRAMES * PR, PC, 2, 2, LAT_CH).transpose(0, 2, 1, 3, 4)
    latent = latent.reshape(FRAMES, 2 * PR, 2 * PC, LAT_CH)
    padded_lat = jnp.pad(latent, ((0, 0), (0, 0), (OV, OV + WMOST), (0, 0)))
    widths = tile_widths.astype(jnp.int32)
    starts = (jnp.cumsum(widths) - widths).astype(jnp.int32)
    pix_cols = 4 * PC
    canvas = jnp.zeros((FRAMES, 4 * PR, pix_cols + 4 * TW, CH_OUT), jnp.float32)
    positions = jnp.arange(2 * TW, dtype=jnp.int32)
    denom = jnp.zeros((pix_cols,), jnp.float32)
    every_col = jnp.arange(pix_cols, dtype=jnp.int32)
    for tile in range(N_TILE):
        begin = starts[tile]
        window = lax.dynamic_slice_in_dim(padded_lat, begin, TW, 2)
        keep = (jnp.arange(TW, dtype=jnp.int32) < widths[tile] + 2 * OV).astype(jnp.float32)
        window = (window.astype(jnp.float32) * keep[None, None, :, None]).astype(jnp.bfloat16)
        extended = jnp.concatenate([jnp.zeros((2,) + window.shape[1:], jnp.bfloat16), window], axis=0)
        tile_out = up_block(extended, keep, conv_in_weight, conv_in_bias, conv_up_weight, conv_up_bias)
        pix_begin = (2 * (begin - OV)).astype(jnp.int32)
        span = (2 * (widths[tile] + 2 * OV)).astype(jnp.int32)
        weight = ramp(pix_begin + positions, pix_begin, span)
        contrib = tile_out.astype(jnp.float32) * weight[None, None, :, None]
        offset = (pix_begin + 2 * TW).astype(jnp.int32)
        current = lax.dynamic_slice_in_dim(canvas, offset, 2 * TW, 2)
        canvas = lax.dynamic_update_slice_in_dim(canvas, current + contrib, offset, 2)
        denom = denom + ramp(every_col, pix_begin, span)
    blended = canvas[:, :, 2 * TW:2 * TW + pix_cols]
    return (blended / denom[None, None, :, None]).astype(jnp.bfloat16)
```

```python
import functools

import jax
import jax.numpy as jnp
from jax import lax
from jax.experimental import pallas as pl
from jax.experimental.pallas import tpu as pltpu
from jax.sharding import PartitionSpec as P

HD = 128
PR = 16
PC = 32
OV = 2
CB = 8
QB = 256
GROUPS = 4
VMEM_LIMIT = 56 * 1024 * 1024
MESH = pl.DeviceIdType.MESH


def attention_kernel(
    dims,
    q_ref,
    k_ref,
    v_ref,
    shift_ref,
    scale_ref,
    fw_ref,
    fb_ref,
    lat_ref,
    q_buf,
    k_buf,
    v_buf,
    top,
    acc,
    o_buf,
    att,
    out_patch,
    in_patch,
    local_sem,
    send_sem,
    recv_sem,
    relay_send,
    relay_recv,
    patch_send,
    patch_recv,
):
    heads, nseq, ntile, needed, own = dims
    ndev = nseq * ntile
    members = ndev // heads
    count = q_ref.shape[0]
    s = lax.axis_index("seq")
    t = lax.axis_index("tile")
    me = s * ntile + t
    rank = lax.div(me, members)
    side = lax.rem(me, members)

    def place(device):
        return (lax.div(device, ntile), lax.rem(device, ntile))

    def peer(r):
        return place(lax.rem(r + heads, heads) * members + side)

    def columns(h):
        return pl.ds(pl.multiple_of(h * HD, HD), HD)

    barrier = pltpu.get_barrier_semaphore()

    @pl.loop(1, ndev)
    def _(i):
        pl.semaphore_signal(
            barrier, inc=1, device_id=place(lax.rem(me + i, ndev)), device_id_type=MESH
        )

    pl.semaphore_wait(barrier, ndev - 1)

    targets = (
        lambda off: q_buf.at[off],
        lambda off: k_buf.at[side, off],
        lambda off: v_buf.at[side, off, :, 0:HD],
    )
    sources = (q_ref, k_ref, v_ref)

    def outgoing(kind, off):
        h = lax.rem(rank + off, heads)
        return pltpu.make_async_remote_copy(
            src_ref=sources[kind].at[:, columns(h)],
            dst_ref=targets[kind](off),
            send_sem=send_sem.at[kind, off],
            recv_sem=recv_sem.at[kind, off],
            device_id=peer(rank + off),
            device_id_type=MESH,
        )

    locals_ = [
        pltpu.make_async_copy(
            sources[kind].at[:, columns(rank)], targets[kind](0), local_sem.at[kind]
        )
        for kind in range(3)
    ]
    for copy in locals_:
        copy.start()

    @pl.loop(1, heads)
    def _(off):
        outgoing(0, off).start()

    @pl.loop(1, heads)
    def _(off):
        outgoing(1, off).start()
        outgoing(2, off).start()

    v_buf[:, :, :, HD:] = jnp.ones_like(v_buf[:, :, :, HD:])
    top[...] = jnp.full_like(top, -1e30)
    acc[...] = jnp.zeros_like(acc)
    for copy in locals_:
        copy.wait()

    @pl.loop(1, heads)
    def _(off):
        outgoing(0, off).wait_recv()

    def relay(kind, part, other):
        slots = pl.ds(part * per, per)
        ref = (None, k_buf.at[side, slots], v_buf.at[side, slots, :, 0:HD])[kind]
        return pltpu.make_async_remote_copy(
            src_ref=ref,
            dst_ref=ref,
            send_sem=relay_send.at[kind - 1, part, other],
            recv_sem=relay_recv.at[kind - 1, part, other],
            device_id=place(rank * members + lax.rem(side + other, members)),
            device_id_type=MESH,
        )

    def relayed(kind, part, other):
        slots = pl.ds(part * per, per)
        origin = lax.rem(side - other + members, members)
        ref = (None, k_buf.at[origin, slots], v_buf.at[origin, slots, :, 0:HD])[kind]
        return pltpu.make_async_remote_copy(
            src_ref=ref,
            dst_ref=ref,
            send_sem=relay_send.at[kind - 1, part, other],
            recv_sem=relay_recv.at[kind - 1, part, other],
            device_id=place(rank * members + lax.rem(side + other, members)),
            device_id_type=MESH,
        )

    def give_back(off):
        return pltpu.make_async_remote_copy(
            src_ref=o_buf.at[off],
            dst_ref=att.at[rank],
            send_sem=send_sem.at[3, off],
            recv_sem=recv_sem.at[3, off],
            device_id=peer(rank - off),
            device_id_type=MESH,
        )

    def returned(off):
        return pltpu.make_async_remote_copy(
            src_ref=o_buf.at[off],
            dst_ref=att.at[lax.rem(rank + off, heads)],
            send_sem=send_sem.at[3, off],
            recv_sem=recv_sem.at[3, off],
            device_id=peer(rank - off),
            device_id_type=MESH,
        )

    per = heads // GROUPS
    factor = HD**-0.5 * 1.4426950408889634
    width = QB // count
    for part in range(GROUPS):
        first = max(part * per, 1)

        @pl.loop(first, (part + 1) * per)
        def _(off):
            outgoing(1, off).wait_recv()
            outgoing(2, off).wait_recv()

        for other in range(1, members):
            relay(1, part, other).start()
            relay(2, part, other).start()
        for other in range(1, members):
            relayed(1, part, other).wait_recv()
            relayed(2, part, other).wait_recv()

        @pl.loop(0, heads // width)
        def _(i):
            rows = pl.ds(pl.multiple_of(i * QB, QB), QB)
            q = q_buf[pl.ds(i * width, width)].reshape(QB, HD)
            keys = k_buf[:, part * per : (part + 1) * per].reshape(-1, HD)
            vals = v_buf[:, part * per : (part + 1) * per].reshape(-1, 2 * HD)
            scores = lax.dot_general(
                q, keys, (((1,), (1,)), ((), ())), preferred_element_type=jnp.float32
            )
            old = top[rows, :]
            new = jnp.maximum(old, jnp.max(scores, axis=1, keepdims=True))
            probs = jnp.exp2((scores - new[:, 0:1]) * factor).astype(jnp.bfloat16)
            fade = jnp.exp2((old - new) * factor)
            total = acc[rows, :] * jnp.concatenate([fade, fade], axis=1) + jnp.dot(
                probs, vals, preferred_element_type=jnp.float32
            )
            if part < GROUPS - 1:
                top[rows, :] = new
                acc[rows, :] = total
            else:
                o = (total[:, 0:HD] / total[:, HD:]).astype(jnp.bfloat16)
                o_buf[pl.ds(i * width, width)] = o.reshape(width, count, HD)
                for j in range(width):
                    off = i * width + j

                    @pl.when(off > 0)
                    def _():
                        give_back(off).start()

    att[rank] = o_buf[0]

    @pl.loop(1, heads)
    def _(off):
        returned(off).wait_recv()

    feats = [att[h].astype(jnp.float32) for h in range(heads)]
    mean = jnp.sum(sum(feats), axis=1, keepdims=True) / (heads * HD)
    devs = [x - mean for x in feats]
    var = jnp.sum(sum(d * d for d in devs), axis=1, keepdims=True) / (heads * HD)
    inv = 1.0 / jnp.sqrt(var + 1e-06)
    normed = jnp.concatenate(
        [
            devs[h] * inv * (1.0 + scale_ref[h : h + 1, :]) + shift_ref[h : h + 1, :]
            for h in range(heads)
        ],
        axis=1,
    )
    patches = (
        jnp.dot(
            normed,
            fw_ref[...],
            precision=lax.Precision.HIGHEST,
            preferred_element_type=jnp.float32,
        )
        + fb_ref[...]
    )
    patches = jnp.concatenate([patches, patches], axis=1)
    col = lax.rem(lax.broadcasted_iota(jnp.int32, patches.shape, 0), PC)
    shifted = (
        jnp.where(col == 0, 0.0, pltpu.roll(patches, 1, 0)),
        patches,
        jnp.where(col == PC - 1, 0.0, pltpu.roll(patches, count - 1, 0)),
    )
    lines = count // PC
    for sh in range(3):
        grid = shifted[sh].reshape(lines, PC, 2 * 64)
        if own < CB:
            grid = jnp.concatenate([grid, jnp.zeros((lines, CB, 2 * 64), jnp.float32)], axis=1)
        for tp in range(ntile):
            out_patch[tp, sh] = (
                grid[:, own * tp : own * tp + CB].reshape(lines * CB, 2 * 64).astype(jnp.bfloat16)
            )

    def patch_copy(dist, step, incoming=False):
        tp = lax.rem(t + step, ntile)
        origin = lax.rem(t - step + ntile, ntile) if incoming else t
        return pltpu.make_async_remote_copy(
            src_ref=out_patch.at[tp],
            dst_ref=in_patch.at[needed - dist, origin],
            send_sem=patch_send.at[dist, step],
            recv_sem=patch_recv.at[dist, step],
            device_id=(lax.rem(s + dist, nseq), tp),
            device_id_type=MESH,
        )

    for dist in reversed(range(needed + 1)):

        @pl.when(s + dist < nseq)
        def _():
            @pl.loop(0 if dist else 1, ntile)
            def _(step):
                patch_copy(dist, step).start()

    in_patch[needed, t] = out_patch[t]
    for dist in range(needed + 1):

        @pl.when(s >= dist)
        def _():
            @pl.loop(0 if dist else 1, ntile)
            def _(step):
                patch_copy(dist, step, True).wait_recv()

            lat_ref[needed - dist] = in_patch[needed - dist]

        @pl.when(s < dist)
        def _():
            lat_ref[needed - dist] = jnp.zeros_like(lat_ref[needed - dist])

    @pl.loop(1, heads)
    def _(off):
        for kind in range(3):
            outgoing(kind, off).wait_send()
        give_back(off).wait_send()

    for part in range(GROUPS):
        for other in range(1, members):
            relay(1, part, other).wait_send()
            relay(2, part, other).wait_send()
    for dist in range(needed + 1):

        @pl.when(s + dist < nseq)
        def _():
            @pl.loop(0 if dist else 1, ntile)
            def _(step):
                patch_copy(dist, step).wait_send()


def prepare_weights(win_ref, wup_ref, wx, wph):
    wx[...] = jnp.zeros_like(wx)
    for a in range(2):
        for b in range(2):
            for kx in range(3):
                half = (b + kx - 1) % 2
                for kt in range(3):
                    for i in range(2):
                        for line in range(2):
                            ky = 2 * (i - 1 + a) + line - a + 1
                            if 0 <= ky <= 2:
                                to = kt * 128 + i * 64 + (line * 2 + half) * 16
                                at = ((kt * 3 + ky) * 3 + kx) * 16
                                wx[a, b, kx, to : to + 16, :] = win_ref[at : at + 16, :]
    taps = (((0,), (1, 2)), ((0, 1), (2,)))
    for a in range(2):
        for b in range(2):
            for ty in range(2):
                for tx in range(2):
                    parts = [
                        wup_ref[ky * 3 + kx].astype(jnp.float32)
                        for ky in taps[a][ty]
                        for kx in taps[b][tx]
                    ]
                    wph[a, b, ty * 2 + tx] = sum(parts[1:], parts[0]).astype(jnp.bfloat16)


def conv_kernel(
    dims,
    tile_ref,
    widths_ref,
    lat_ref,
    win_ref,
    bin_ref,
    wup_ref,
    bup_ref,
    out_ref,
    wx,
    wph,
    mixed,
    wide,
    hidden,
    coef,
    cut,
):
    ntile, frames, lines, own = dims
    t = tile_ref[0]
    prepare_weights(win_ref, wup_ref, wx, wph)

    col = lax.broadcasted_iota(jnp.int32, (CB, 128), 0) + own * t
    starts, spans = [], []
    begin = jnp.int32(0)
    for k in range(ntile):
        starts.append(begin - OV)
        spans.append(widths_ref[k] + 2 * OV)
        begin = begin + widths_ref[k]
    for b in range(2):
        for px in range(2):
            x = 4 * col + 2 * b + px
            ramps = []
            for k in range(ntile):
                u = x - 2 * starts[k]
                dist = jnp.minimum(u, 2 * spans[k] - 1 - u) + 1
                ramps.append(jnp.clip(dist, 0, 4 * OV).astype(jnp.float32))
            scale = 1.0 / sum(ramps)
            for tx in range(2):
                full = left = right = jnp.zeros((CB, 128), jnp.float32)
                for k in range(ntile):
                    j = 2 * col + b + tx - 1 + px - starts[k]
                    share = ramps[k] * scale
                    left = left + jnp.where(j == 0, share, 0.0)
                    right = right + jnp.where(j == spans[k] - 1, share, 0.0)
                    full = full + jnp.where((j > 0) & (j < spans[k] - 1), share, 0.0)
                for v, c in enumerate((full, left, right)):
                    coef[b, px, tx, v] = c

    rows = PR * CB
    cut[...] = jnp.zeros_like(cut)
    lane = lax.broadcasted_iota(jnp.int32, (rows, 128), 1)
    blocks = PR // lines
    pad = jnp.zeros((CB, 128), jnp.float32)

    for frame in range(frames):
        first = lat_ref.shape[0] * frames - frames - 2 + frame
        for sh in range(3):
            pieces = ([], [])
            for kt in range(3):
                slot, inner = divmod(first + kt, frames)
                x = jnp.concatenate(
                    [lat_ref[slot, inner * blocks + i, sh] for i in range(blocks)], axis=0
                ).astype(jnp.float32)
                above = jnp.concatenate([pad, x[:-CB]], axis=0)
                below = jnp.concatenate([x[CB:], pad], axis=0)
                pieces[0].append(jnp.where(lane < 64, above, x).astype(jnp.bfloat16))
                pieces[1].append(jnp.where(lane < 64, x, below).astype(jnp.bfloat16))
            for a in range(2):
                cut[a, sh] = jnp.concatenate(pieces[a], axis=1)

        for a in range(2):
            for b in range(2):
                for kx in range(3):
                    low = (b + kx - 1) // 2 + 1 - b
                    source = jnp.concatenate([cut[a, low], cut[a, low + 1]], axis=0)
                    hidden[kx] = jnp.dot(
                        source, wx[a, b, kx], preferred_element_type=jnp.float32
                    ).reshape(2, PR, CB, -1)

                @pl.loop(0, PR)
                def _(r):
                    left, middle, right = (hidden[kx, :, r] for kx in range(3))
                    middle = middle + bin_ref[...][None]
                    hidden[0, :, r] = jax.nn.silu(left + middle + right)
                    hidden[1, :, r] = jax.nn.silu(middle + right)
                    hidden[2, :, r] = jax.nn.silu(left + middle)

                for hi in range(2):
                    place = 2 * hi - b
                    for ob in range(2):
                        for px in range(2):
                            tx = place + 1 - ob - px
                            if tx not in (0, 1):
                                continue
                            for part in range(0, hidden.shape[-1], 128):
                                lanes = slice(part, part + 128)
                                value = hidden[0, hi, :, :, lanes] * coef[ob, px, tx, 0][None]
                                for v in (1, 2):
                                    value = (
                                        value
                                        + hidden[v, hi, :, :, lanes] * coef[ob, px, tx, v][None]
                                    )
                                gone = jnp.zeros((1,) + value.shape[1:], jnp.float32)
                                if a == 0:
                                    moved = jnp.concatenate([value[1:], gone], axis=0)
                                    spots = (1, 3)
                                else:
                                    moved = jnp.concatenate([gone, value[:-1]], axis=0)
                                    spots = (2, 0)
                                for spot, val in zip(spots, (value, moved)):
                                    mixed[ob, px, tx, spot, :, lanes] = val.reshape(
                                        rows, 128
                                    ).astype(jnp.bfloat16)

        for ya in range(2):
            for px in range(2):
                total = None
                for ty in range(2):
                    for tx in range(2):
                        source = jnp.concatenate(
                            [
                                mixed[b, px, tx, a + ty + ya]
                                for a in range(2)
                                for b in range(2)
                            ],
                            axis=0,
                        )
                        term = jnp.dot(
                            source, wph[ya, px, ty * 2 + tx], preferred_element_type=jnp.float32
                        )
                        total = term if total is None else total + term
                total = (total + bup_ref[...]).reshape(2, 2, PR, CB, -1)
                for a in range(2):
                    for b in range(2):
                        for half in range(2):
                            wide[
                                half, :, 2 * a + ya, pl.ds(2 * b + px, CB, stride=4), :
                            ] = total[a, b, :, :, half * 128 : (half + 1) * 128]
        for half in range(2):
            out_ref[frame, :, :, half * 128 : (half + 1) * 128] = (
                wide[half, :, :, 0 : 4 * own, :]
                .reshape(4 * PR, 4 * own, -1)
                .astype(jnp.bfloat16)
            )


def per_device(
    queries,
    keys,
    values,
    mod_shift,
    mod_scale,
    final_weight,
    final_bias,
    tile_widths,
    conv_in_weight,
    conv_in_bias,
    conv_up_weight,
    conv_up_bias,
):
    nseq, ntile = lax.axis_size("seq"), lax.axis_size("tile")
    count, feat = queries.shape
    heads = feat // HD
    ndev = nseq * ntile
    members = ndev // heads
    lines = count // PC
    frames = count * ntile // (PR * PC)
    needed = -(-2 // frames)
    own = PC // ntile
    vmem = pl.BlockSpec(memory_space=pltpu.VMEM)
    lat_shape = (needed + 1, ntile, 3, lines * CB, 128)
    lat = pl.pallas_call(
        functools.partial(attention_kernel, (heads, nseq, ntile, needed, own)),
        out_shape=jax.ShapeDtypeStruct(lat_shape, jnp.bfloat16),
        in_specs=[vmem] * 7,
        out_specs=vmem,
        scratch_shapes=[
            pltpu.VMEM((heads, count, HD), jnp.bfloat16),
            pltpu.VMEM((members, heads, count, HD), jnp.bfloat16),
            pltpu.VMEM((members, heads, count, 2 * HD), jnp.bfloat16),
            pltpu.VMEM((heads * count, HD), jnp.float32),
            pltpu.VMEM((heads * count, 2 * HD), jnp.float32),
            pltpu.VMEM((heads, count, HD), jnp.bfloat16),
            pltpu.VMEM((heads, count, HD), jnp.bfloat16),
            pltpu.VMEM(lat_shape[1:], jnp.bfloat16),
            pltpu.VMEM(lat_shape, jnp.bfloat16),
            pltpu.SemaphoreType.DMA((3,)),
            pltpu.SemaphoreType.DMA((4, heads)),
            pltpu.SemaphoreType.DMA((4, heads)),
            pltpu.SemaphoreType.DMA((2, GROUPS, members)),
            pltpu.SemaphoreType.DMA((2, GROUPS, members)),
            pltpu.SemaphoreType.DMA((needed + 1, ntile)),
            pltpu.SemaphoreType.DMA((needed + 1, ntile)),
        ],
        compiler_params=pltpu.CompilerParams(
            collective_id=0, has_side_effects=True, vmem_limit_bytes=VMEM_LIMIT
        ),
    )(
        queries,
        keys,
        values,
        mod_shift.reshape(heads, HD),
        mod_scale.reshape(heads, HD),
        final_weight,
        final_bias.reshape(1, -1),
    )
    ch_in, ch_out = conv_up_weight.shape[1:]
    return pl.pallas_call(
        functools.partial(conv_kernel, (ntile, frames, lines, own)),
        out_shape=jax.ShapeDtypeStruct((frames, 4 * PR, 4 * own, ch_out), jnp.bfloat16),
        in_specs=[pl.BlockSpec(memory_space=pltpu.SMEM)] * 2 + [vmem] * 5,
        out_specs=vmem,
        scratch_shapes=[
            pltpu.VMEM((2, 2, 3, 384, ch_in), jnp.bfloat16),
            pltpu.VMEM((2, 2, 4, ch_in, ch_out), jnp.bfloat16),
            pltpu.VMEM((2, 2, 2, 4, PR * CB, ch_in), jnp.bfloat16),
            pltpu.VMEM((2, PR, 4, 4 * CB, 128), jnp.float32),
            pltpu.VMEM((3, 2, PR, CB, ch_in), jnp.float32),
            pltpu.VMEM((2, 2, 2, 3, CB, 128), jnp.float32),
            pltpu.VMEM((2, 3, PR * CB, 384), jnp.bfloat16),
        ],
        compiler_params=pltpu.CompilerParams(vmem_limit_bytes=VMEM_LIMIT),
    )(
        lax.axis_index("tile").reshape(1),
        tile_widths,
        lat,
        conv_in_weight,
        conv_in_bias.reshape(1, -1),
        conv_up_weight,
        conv_up_bias.reshape(1, -1),
    )


def solution(mesh):
    return jax.shard_map(
        per_device,
        mesh=mesh,
        in_specs=(P(("seq", "tile"), None),) * 3 + (P(),) * 9,
        out_specs=P("seq", None, "tile", None),
        check_vma=False,
    )
```

```python
import functools

import jax
import jax.numpy as jnp
from jax import lax
from jax.experimental import pallas as pl
from jax.experimental.pallas import tpu as pltpu
from jax.sharding import PartitionSpec as P

HD = 128
PR = 16
PC = 32
OV = 2
CB = 8
QB = 256
GROUPS = 4
VMEM_LIMIT = 56 * 1024 * 1024
MESH = pl.DeviceIdType.MESH


def attention_kernel(
    dims,
    q_ref,
    k_ref,
    v_ref,
    shift_ref,
    scale_ref,
    fw_ref,
    fb_ref,
    lat_ref,
    q_buf,
    k_buf,
    v_buf,
    top,
    acc,
    o_buf,
    att,
    out_patch,
    in_patch,
    local_sem,
    send_sem,
    recv_sem,
    relay_send,
    relay_recv,
    patch_send,
    patch_recv,
):
    heads, nseq, ntile, needed, own = dims
    ndev = nseq * ntile
    members = ndev // heads
    count = q_ref.shape[0]
    s = lax.axis_index("seq")
    t = lax.axis_index("tile")
    me = s * ntile + t
    rank = lax.div(me, members)
    side = lax.rem(me, members)

    def place(device):
        return (lax.div(device, ntile), lax.rem(device, ntile))

    def peer(r):
        return place(lax.rem(r + heads, heads) * members + side)

    def mixed(x, y):
        bits = heads.bit_length() - 1
        return sum(
            lax.rem(lax.div(x, 1 << i) + lax.div(y, 1 << i), 2) * (1 << i) for i in range(bits)
        )

    def columns(h):
        return pl.ds(pl.multiple_of(h * HD, HD), HD)

    barrier = pltpu.get_barrier_semaphore()

    @pl.loop(1, ndev)
    def _(i):
        pl.semaphore_signal(
            barrier, inc=1, device_id=place(lax.rem(me + i, ndev)), device_id_type=MESH
        )

    pl.semaphore_wait(barrier, ndev - 1)

    targets = (
        lambda off: q_buf.at[off],
        lambda off: k_buf.at[side, off],
        lambda off: v_buf.at[side, off, :, 0:HD],
    )
    sources = (q_ref, k_ref, v_ref)

    def outgoing(kind, off):
        h = mixed(rank, off)
        return pltpu.make_async_remote_copy(
            src_ref=sources[kind].at[:, columns(h)],
            dst_ref=targets[kind](off),
            send_sem=send_sem.at[kind, off],
            recv_sem=recv_sem.at[kind, off],
            device_id=peer(mixed(rank, off)),
            device_id_type=MESH,
        )

    locals_ = [
        pltpu.make_async_copy(
            sources[kind].at[:, columns(rank)], targets[kind](0), local_sem.at[kind]
        )
        for kind in range(3)
    ]
    for copy in locals_:
        copy.start()

    @pl.loop(1, heads)
    def _(o):
        off = heads - o
        outgoing(0, off).start()

    @pl.loop(1, heads)
    def _(off):
        outgoing(1, off).start()
        outgoing(2, off).start()

    v_buf[:, :, :, HD:] = jnp.ones_like(v_buf[:, :, :, HD:])
    top[...] = jnp.full_like(top, -1e30)
    acc[...] = jnp.zeros_like(acc)
    for copy in locals_:
        copy.wait()

    @pl.loop(1, heads)
    def _(off):
        outgoing(0, off).wait_recv()

    def relay(kind, part, other):
        slots = pl.ds(part * per, per)
        ref = (None, k_buf.at[side, slots], v_buf.at[side, slots, :, 0:HD])[kind]
        return pltpu.make_async_remote_copy(
            src_ref=ref,
            dst_ref=ref,
            send_sem=relay_send.at[kind - 1, part, other],
            recv_sem=relay_recv.at[kind - 1, part, other],
            device_id=place(rank * members + lax.rem(side + other, members)),
            device_id_type=MESH,
        )

    def relayed(kind, part, other):
        slots = pl.ds(part * per, per)
        origin = lax.rem(side - other + members, members)
        ref = (None, k_buf.at[origin, slots], v_buf.at[origin, slots, :, 0:HD])[kind]
        return pltpu.make_async_remote_copy(
            src_ref=ref,
            dst_ref=ref,
            send_sem=relay_send.at[kind - 1, part, other],
            recv_sem=relay_recv.at[kind - 1, part, other],
            device_id=place(rank * members + lax.rem(side + other, members)),
            device_id_type=MESH,
        )

    def give_back(off):
        return pltpu.make_async_remote_copy(
            src_ref=o_buf.at[off],
            dst_ref=att.at[rank],
            send_sem=send_sem.at[3, off],
            recv_sem=recv_sem.at[3, off],
            device_id=peer(mixed(rank, off)),
            device_id_type=MESH,
        )

    def returned(off):
        return pltpu.make_async_remote_copy(
            src_ref=o_buf.at[off],
            dst_ref=att.at[mixed(rank, off)],
            send_sem=send_sem.at[3, off],
            recv_sem=recv_sem.at[3, off],
            device_id=peer(mixed(rank, off)),
            device_id_type=MESH,
        )

    per = heads // GROUPS
    factor = HD**-0.5 * 1.4426950408889634
    width = QB // count
    for part in range(GROUPS):
        first = max(part * per, 1)

        @pl.loop(first, (part + 1) * per)
        def _(off):
            outgoing(1, off).wait_recv()
            outgoing(2, off).wait_recv()

        for other in range(1, members):
            relay(1, part, other).start()
            relay(2, part, other).start()
        for other in range(1, members):
            relayed(1, part, other).wait_recv()
            relayed(2, part, other).wait_recv()

        @pl.loop(0, heads // width, unroll=2)
        def _(i):
            rows = pl.ds(pl.multiple_of(i * QB, QB), QB)
            q = q_buf[pl.ds(i * width, width)].reshape(QB, HD)
            keys = k_buf[:, part * per : (part + 1) * per].reshape(-1, HD)
            vals = v_buf[:, part * per : (part + 1) * per].reshape(-1, 2 * HD)
            scores = lax.dot_general(
                q, keys, (((1,), (1,)), ((), ())), preferred_element_type=jnp.float32
            )
            old = top[rows, :]
            new = jnp.maximum(old, jnp.max(scores, axis=1, keepdims=True))
            probs = jnp.exp2((scores - new[:, 0:1]) * factor).astype(jnp.bfloat16)
            fade = jnp.exp2((old - new) * factor)
            total = acc[rows, :] * jnp.concatenate([fade, fade], axis=1) + jnp.dot(
                probs, vals, preferred_element_type=jnp.float32
            )
            if part < GROUPS - 1:
                top[rows, :] = new
                acc[rows, :] = total
            else:
                o = (total[:, 0:HD] / total[:, HD:]).astype(jnp.bfloat16)
                o_buf[pl.ds(i * width, width)] = o.reshape(width, count, HD)
                for j in range(width):
                    off = i * width + j

                    @pl.when(off > 0)
                    def _():
                        give_back(off).start()

    att[rank] = o_buf[0]

    @pl.loop(1, heads)
    def _(off):
        returned(off).wait_recv()

    feats = [att[h].astype(jnp.float32) for h in range(heads)]
    mean = jnp.sum(sum(feats), axis=1, keepdims=True) / (heads * HD)
    devs = [x - mean for x in feats]
    var = jnp.sum(sum(d * d for d in devs), axis=1, keepdims=True) / (heads * HD)
    inv = 1.0 / jnp.sqrt(var + 1e-06)
    normed = jnp.concatenate(
        [
            devs[h] * inv * (1.0 + scale_ref[h : h + 1, :]) + shift_ref[h : h + 1, :]
            for h in range(heads)
        ],
        axis=1,
    )
    patches = (
        lax.dot_general(
            normed,
            fw_ref[...],
            (((1,), (1,)), ((), ())),
            precision=lax.Precision.HIGHEST,
            preferred_element_type=jnp.float32,
        )
        + fb_ref[...]
    )
    patches = jnp.concatenate([patches, patches], axis=1)
    col = lax.rem(lax.broadcasted_iota(jnp.int32, patches.shape, 0), PC)
    shifted = (
        jnp.where(col == 0, 0.0, pltpu.roll(patches, 1, 0)),
        patches,
        jnp.where(col == PC - 1, 0.0, pltpu.roll(patches, count - 1, 0)),
    )
    lines = count // PC
    for sh in range(3):
        grid = shifted[sh].reshape(lines, PC, 2 * 64)
        if own < CB:
            grid = jnp.concatenate([grid, jnp.zeros((lines, CB, 2 * 64), jnp.float32)], axis=1)
        for tp in range(ntile):
            out_patch[tp, sh] = (
                grid[:, own * tp : own * tp + CB].reshape(lines * CB, 2 * 64).astype(jnp.bfloat16)
            )

    def patch_copy(dist, step, incoming=False):
        tp = lax.rem(t + step, ntile)
        origin = lax.rem(t - step + ntile, ntile) if incoming else t
        return pltpu.make_async_remote_copy(
            src_ref=out_patch.at[tp],
            dst_ref=in_patch.at[needed - dist, origin],
            send_sem=patch_send.at[dist, step],
            recv_sem=patch_recv.at[dist, step],
            device_id=(lax.rem(s + dist, nseq), tp),
            device_id_type=MESH,
        )

    for dist in reversed(range(needed + 1)):

        @pl.when(s + dist < nseq)
        def _():
            @pl.loop(0 if dist else 1, ntile)
            def _(step):
                patch_copy(dist, step).start()

    in_patch[needed, t] = out_patch[t]
    for dist in range(needed + 1):

        @pl.when(s >= dist)
        def _():
            @pl.loop(0 if dist else 1, ntile)
            def _(step):
                patch_copy(dist, step, True).wait_recv()

            lat_ref[needed - dist] = in_patch[needed - dist]

        @pl.when(s < dist)
        def _():
            lat_ref[needed - dist] = jnp.zeros_like(lat_ref[needed - dist])

    @pl.loop(1, heads)
    def _(off):
        for kind in range(3):
            outgoing(kind, off).wait_send()
        give_back(off).wait_send()

    for part in range(GROUPS):
        for other in range(1, members):
            relay(1, part, other).wait_send()
            relay(2, part, other).wait_send()
    for dist in range(needed + 1):

        @pl.when(s + dist < nseq)
        def _():
            @pl.loop(0 if dist else 1, ntile)
            def _(step):
                patch_copy(dist, step).wait_send()


def prepare_weights(win_ref, wup_ref, wx, wph):
    wx[...] = jnp.zeros_like(wx)
    for a in range(2):
        for b in range(2):
            for kx in range(3):
                half = (b + kx - 1) % 2
                for kt in range(3):
                    for i in range(2):
                        for line in range(2):
                            ky = 2 * (i - 1 + a) + line - a + 1
                            if 0 <= ky <= 2:
                                to = kt * 128 + i * 64 + (line * 2 + half) * 16
                                at = ((kt * 3 + ky) * 3 + kx) * 16
                                wx[a, b, kx, to : to + 16, :] = win_ref[at : at + 16, :]
    taps = (((0,), (1, 2)), ((0, 1), (2,)))
    for a in range(2):
        for b in range(2):
            for ty in range(2):
                for tx in range(2):
                    parts = [
                        wup_ref[ky * 3 + kx].astype(jnp.float32)
                        for ky in taps[a][ty]
                        for kx in taps[b][tx]
                    ]
                    wph[a, b, ty * 2 + tx] = sum(parts[1:], parts[0]).astype(jnp.bfloat16)


def conv_kernel(
    dims,
    tile_ref,
    widths_ref,
    lat_ref,
    win_ref,
    bin_ref,
    wup_ref,
    bup_ref,
    out_ref,
    wx,
    wph,
    mixed,
    wide,
    hidden,
    coef,
    cut,
):
    ntile, frames, lines, own = dims
    t = tile_ref[0]
    prepare_weights(win_ref, wup_ref, wx, wph)

    col = lax.broadcasted_iota(jnp.int32, (CB, 128), 0) + own * t
    starts, spans = [], []
    begin = jnp.int32(0)
    for k in range(ntile):
        starts.append(begin - OV)
        spans.append(widths_ref[k] + 2 * OV)
        begin = begin + widths_ref[k]
    for b in range(2):
        for px in range(2):
            x = 4 * col + 2 * b + px
            ramps = []
            for k in range(ntile):
                u = x - 2 * starts[k]
                dist = jnp.minimum(u, 2 * spans[k] - 1 - u) + 1
                ramps.append(jnp.clip(dist, 0, 4 * OV).astype(jnp.float32))
            scale = 1.0 / sum(ramps)
            for tx in range(2):
                full = left = right = jnp.zeros((CB, 128), jnp.float32)
                for k in range(ntile):
                    j = 2 * col + b + tx - 1 + px - starts[k]
                    share = ramps[k] * scale
                    left = left + jnp.where(j == 0, share, 0.0)
                    right = right + jnp.where(j == spans[k] - 1, share, 0.0)
                    full = full + jnp.where((j > 0) & (j < spans[k] - 1), share, 0.0)
                for v, c in enumerate((full, left, right)):
                    coef[b, px, tx, v] = c

    rows = PR * CB
    cut[...] = jnp.zeros_like(cut)
    lane = lax.broadcasted_iota(jnp.int32, (rows, 128), 1)
    blocks = PR // lines
    pad = jnp.zeros((CB, 128), jnp.float32)

    for frame in range(frames):
        first = lat_ref.shape[0] * frames - frames - 2 + frame
        for sh in range(3):
            pieces = ([], [])
            for kt in range(3):
                slot, inner = divmod(first + kt, frames)
                x = jnp.concatenate(
                    [lat_ref[slot, inner * blocks + i, sh] for i in range(blocks)], axis=0
                ).astype(jnp.float32)
                above = jnp.concatenate([pad, x[:-CB]], axis=0)
                below = jnp.concatenate([x[CB:], pad], axis=0)
                pieces[0].append(jnp.where(lane < 64, above, x).astype(jnp.bfloat16))
                pieces[1].append(jnp.where(lane < 64, x, below).astype(jnp.bfloat16))
            for a in range(2):
                cut[a, sh] = jnp.concatenate(pieces[a], axis=1)

        for a in range(2):
            for b in range(2):
                for kx in range(3):
                    low = (b + kx - 1) // 2 + 1 - b
                    source = jnp.concatenate([cut[a, low], cut[a, low + 1]], axis=0)
                    hidden[kx] = jnp.dot(
                        source, wx[a, b, kx], preferred_element_type=jnp.float32
                    ).reshape(2, PR, CB, -1)

                @pl.loop(0, PR)
                def _(r):
                    left, middle, right = (hidden[kx, :, r] for kx in range(3))
                    middle = middle + bin_ref[...][None]
                    hidden[0, :, r] = jax.nn.silu(left + middle + right)
                    hidden[1, :, r] = jax.nn.silu(middle + right)
                    hidden[2, :, r] = jax.nn.silu(left + middle)

                for hi in range(2):
                    place = 2 * hi - b
                    for ob in range(2):
                        for px in range(2):
                            tx = place + 1 - ob - px
                            if tx not in (0, 1):
                                continue
                            for part in range(0, hidden.shape[-1], 128):
                                lanes = slice(part, part + 128)
                                value = hidden[0, hi, :, :, lanes] * coef[ob, px, tx, 0][None]
                                for v in (1, 2):
                                    value = (
                                        value
                                        + hidden[v, hi, :, :, lanes] * coef[ob, px, tx, v][None]
                                    )
                                gone = jnp.zeros((1,) + value.shape[1:], jnp.float32)
                                if a == 0:
                                    moved = jnp.concatenate([value[1:], gone], axis=0)
                                    spots = (1, 3)
                                else:
                                    moved = jnp.concatenate([gone, value[:-1]], axis=0)
                                    spots = (2, 0)
                                for spot, val in zip(spots, (value, moved)):
                                    mixed[ob, px, tx, spot, :, lanes] = val.reshape(
                                        rows, 128
                                    ).astype(jnp.bfloat16)

        for ya in range(2):
            for px in range(2):
                total = None
                for ty in range(2):
                    for tx in range(2):
                        source = jnp.concatenate(
                            [
                                mixed[b, px, tx, a + ty + ya]
                                for a in range(2)
                                for b in range(2)
                            ],
                            axis=0,
                        )
                        term = jnp.dot(
                            source, wph[ya, px, ty * 2 + tx], preferred_element_type=jnp.float32
                        )
                        total = term if total is None else total + term
                total = (total + bup_ref[...]).reshape(2, 2, PR, CB, -1)
                for a in range(2):
                    for b in range(2):
                        for half in range(2):
                            wide[
                                half, :, 2 * a + ya, pl.ds(2 * b + px, CB, stride=4), :
                            ] = total[a, b, :, :, half * 128 : (half + 1) * 128]
        for half in range(2):
            out_ref[frame, :, :, half * 128 : (half + 1) * 128] = (
                wide[half, :, :, 0 : 4 * own, :]
                .reshape(4 * PR, 4 * own, -1)
                .astype(jnp.bfloat16)
            )


def per_device(
    queries,
    keys,
    values,
    mod_shift,
    mod_scale,
    final_weight,
    final_bias,
    tile_widths,
    conv_in_weight,
    conv_in_bias,
    conv_up_weight,
    conv_up_bias,
):
    nseq, ntile = lax.axis_size("seq"), lax.axis_size("tile")
    count, feat = queries.shape
    heads = feat // HD
    ndev = nseq * ntile
    members = ndev // heads
    lines = count // PC
    frames = count * ntile // (PR * PC)
    needed = -(-2 // frames)
    own = PC // ntile
    vmem = pl.BlockSpec(memory_space=pltpu.VMEM)
    lat_shape = (needed + 1, ntile, 3, lines * CB, 128)
    lat = pl.pallas_call(
        functools.partial(attention_kernel, (heads, nseq, ntile, needed, own)),
        out_shape=jax.ShapeDtypeStruct(lat_shape, jnp.bfloat16),
        in_specs=[vmem] * 7,
        out_specs=vmem,
        scratch_shapes=[
            pltpu.VMEM((heads, count, HD), jnp.bfloat16),
            pltpu.VMEM((members, heads, count, HD), jnp.bfloat16),
            pltpu.VMEM((members, heads, count, 2 * HD), jnp.bfloat16),
            pltpu.VMEM((heads * count, HD), jnp.float32),
            pltpu.VMEM((heads * count, 2 * HD), jnp.float32),
            pltpu.VMEM((heads, count, HD), jnp.bfloat16),
            pltpu.VMEM((heads, count, HD), jnp.bfloat16),
            pltpu.VMEM(lat_shape[1:], jnp.bfloat16),
            pltpu.VMEM(lat_shape, jnp.bfloat16),
            pltpu.SemaphoreType.DMA((3,)),
            pltpu.SemaphoreType.DMA((4, heads)),
            pltpu.SemaphoreType.DMA((4, heads)),
            pltpu.SemaphoreType.DMA((2, GROUPS, members)),
            pltpu.SemaphoreType.DMA((2, GROUPS, members)),
            pltpu.SemaphoreType.DMA((needed + 1, ntile)),
            pltpu.SemaphoreType.DMA((needed + 1, ntile)),
        ],
        compiler_params=pltpu.CompilerParams(
            collective_id=0, has_side_effects=True, vmem_limit_bytes=VMEM_LIMIT
        ),
    )(
        queries,
        keys,
        values,
        mod_shift.reshape(heads, HD),
        mod_scale.reshape(heads, HD),
        final_weight.T,
        final_bias.reshape(1, -1),
    )
    ch_in, ch_out = conv_up_weight.shape[1:]
    return pl.pallas_call(
        functools.partial(conv_kernel, (ntile, frames, lines, own)),
        out_shape=jax.ShapeDtypeStruct((frames, 4 * PR, 4 * own, ch_out), jnp.bfloat16),
        in_specs=[pl.BlockSpec(memory_space=pltpu.SMEM)] * 2 + [vmem] * 5,
        out_specs=vmem,
        scratch_shapes=[
            pltpu.VMEM((2, 2, 3, 384, ch_in), jnp.bfloat16),
            pltpu.VMEM((2, 2, 4, ch_in, ch_out), jnp.bfloat16),
            pltpu.VMEM((2, 2, 2, 4, PR * CB, ch_in), jnp.bfloat16),
            pltpu.VMEM((2, PR, 4, 4 * CB, 128), jnp.float32),
            pltpu.VMEM((3, 2, PR, CB, ch_in), jnp.float32),
            pltpu.VMEM((2, 2, 2, 3, CB, 128), jnp.float32),
            pltpu.VMEM((2, 3, PR * CB, 384), jnp.bfloat16),
        ],
        compiler_params=pltpu.CompilerParams(vmem_limit_bytes=VMEM_LIMIT),
    )(
        lax.axis_index("tile").reshape(1),
        tile_widths,
        lat,
        conv_in_weight,
        conv_in_bias.reshape(1, -1),
        conv_up_weight,
        conv_up_bias.reshape(1, -1),
    )


def solution(mesh):
    return jax.shard_map(
        per_device,
        mesh=mesh,
        in_specs=(P(("seq", "tile"), None),) * 3 + (P(),) * 9,
        out_specs=P("seq", None, "tile", None),
        check_vma=False,
    )
```

```python
import functools

import jax
import jax.numpy as jnp
from jax import lax
from jax.experimental import pallas as pl
from jax.experimental.pallas import tpu as pltpu
from jax.sharding import PartitionSpec as P

HD = 128
PR = 16
PC = 32
OV = 2
CB = 8
QB = 256
GROUPS = 4
VMEM_LIMIT = 56 * 1024 * 1024
MESH = pl.DeviceIdType.MESH


def attention_kernel(
    dims,
    q_ref,
    k_ref,
    v_ref,
    shift_ref,
    scale_ref,
    fw_ref,
    fb_ref,
    lat_ref,
    q_buf,
    k_buf,
    v_buf,
    top,
    acc,
    o_buf,
    att,
    out_patch,
    in_patch,
    local_sem,
    send_sem,
    recv_sem,
    relay_send,
    relay_recv,
    patch_send,
    patch_recv,
):
    heads, nseq, ntile, needed, own = dims
    ndev = nseq * ntile
    members = ndev // heads
    count = q_ref.shape[0]
    s = lax.axis_index("seq")
    t = lax.axis_index("tile")
    me = s * ntile + t
    rank = lax.div(me, members)
    side = lax.rem(me, members)

    def place(device):
        return (lax.div(device, ntile), lax.rem(device, ntile))

    def peer(r):
        return place(lax.rem(r + heads, heads) * members + side)

    def mixed(x, y):
        bits = heads.bit_length() - 1
        return sum(
            lax.rem(lax.div(x, 1 << i) + lax.div(y, 1 << i), 2) * (1 << i) for i in range(bits)
        )

    def columns(h):
        return pl.ds(pl.multiple_of(h * HD, HD), HD)

    barrier = pltpu.get_barrier_semaphore()

    @pl.loop(1, ndev)
    def _(i):
        pl.semaphore_signal(
            barrier, inc=1, device_id=place(lax.rem(me + i, ndev)), device_id_type=MESH
        )

    pl.semaphore_wait(barrier, ndev - 1)

    targets = (
        lambda off: q_buf.at[off],
        lambda off: k_buf.at[side, off],
        lambda off: v_buf.at[side, off, :, 0:HD],
    )
    sources = (q_ref, k_ref, v_ref)

    def outgoing(kind, off):
        h = mixed(rank, off)
        return pltpu.make_async_remote_copy(
            src_ref=sources[kind].at[:, columns(h)],
            dst_ref=targets[kind](off),
            send_sem=send_sem.at[kind, off],
            recv_sem=recv_sem.at[kind, off],
            device_id=peer(mixed(rank, off)),
            device_id_type=MESH,
        )

    locals_ = [
        pltpu.make_async_copy(
            sources[kind].at[:, columns(rank)], targets[kind](0), local_sem.at[kind]
        )
        for kind in range(3)
    ]
    for copy in locals_:
        copy.start()

    @pl.loop(1, heads)
    def _(o):
        off = heads - o
        outgoing(0, off).start()

    @pl.loop(1, heads)
    def _(off):
        outgoing(1, off).start()
        outgoing(2, off).start()

    v_buf[:, :, :, HD:] = jnp.ones_like(v_buf[:, :, :, HD:])
    top[...] = jnp.full_like(top, -1e30)
    acc[...] = jnp.zeros_like(acc)
    for copy in locals_:
        copy.wait()

    @pl.loop(1, heads)
    def _(off):
        outgoing(0, off).wait_recv()

    def relay(kind, part, other):
        slots = pl.ds(part * per, per)
        ref = (None, k_buf.at[side, slots], v_buf.at[side, slots, :, 0:HD])[kind]
        return pltpu.make_async_remote_copy(
            src_ref=ref,
            dst_ref=ref,
            send_sem=relay_send.at[kind - 1, part, other],
            recv_sem=relay_recv.at[kind - 1, part, other],
            device_id=place(rank * members + lax.rem(side + other, members)),
            device_id_type=MESH,
        )

    def relayed(kind, part, other):
        slots = pl.ds(part * per, per)
        origin = lax.rem(side - other + members, members)
        ref = (None, k_buf.at[origin, slots], v_buf.at[origin, slots, :, 0:HD])[kind]
        return pltpu.make_async_remote_copy(
            src_ref=ref,
            dst_ref=ref,
            send_sem=relay_send.at[kind - 1, part, other],
            recv_sem=relay_recv.at[kind - 1, part, other],
            device_id=place(rank * members + lax.rem(side + other, members)),
            device_id_type=MESH,
        )

    def give_back(off):
        return pltpu.make_async_remote_copy(
            src_ref=o_buf.at[off],
            dst_ref=att.at[rank],
            send_sem=send_sem.at[3, off],
            recv_sem=recv_sem.at[3, off],
            device_id=peer(mixed(rank, off)),
            device_id_type=MESH,
        )

    def returned(off):
        return pltpu.make_async_remote_copy(
            src_ref=o_buf.at[off],
            dst_ref=att.at[mixed(rank, off)],
            send_sem=send_sem.at[3, off],
            recv_sem=recv_sem.at[3, off],
            device_id=peer(mixed(rank, off)),
            device_id_type=MESH,
        )

    per = heads // GROUPS
    factor = HD**-0.5 * 1.4426950408889634
    width = QB // count
    for part in range(GROUPS):
        first = max(part * per, 1)

        @pl.loop(first, (part + 1) * per)
        def _(off):
            outgoing(1, off).wait_recv()
            outgoing(2, off).wait_recv()

        for other in range(1, members):
            relay(1, part, other).start()
            relay(2, part, other).start()
        for other in range(1, members):
            relayed(1, part, other).wait_recv()
            relayed(2, part, other).wait_recv()

        @pl.loop(0, heads // width, unroll=2)
        def _(turn):
            i = heads // width - 1 - turn
            rows = pl.ds(pl.multiple_of(i * QB, QB), QB)
            q = q_buf[pl.ds(i * width, width)].reshape(QB, HD)
            keys = k_buf[:, part * per : (part + 1) * per].reshape(-1, HD)
            vals = v_buf[:, part * per : (part + 1) * per].reshape(-1, 2 * HD)
            scores = lax.dot_general(
                q, keys, (((1,), (1,)), ((), ())), preferred_element_type=jnp.float32
            )
            old = top[rows, :]
            new = jnp.maximum(old, jnp.max(scores, axis=1, keepdims=True))
            probs = jnp.exp2((scores - new[:, 0:1]) * factor).astype(jnp.bfloat16)
            fade = jnp.exp2((old - new) * factor)
            total = acc[rows, :] * jnp.concatenate([fade, fade], axis=1) + jnp.dot(
                probs, vals, preferred_element_type=jnp.float32
            )
            if part < GROUPS - 1:
                top[rows, :] = new
                acc[rows, :] = total
            else:
                o = (total[:, 0:HD] / total[:, HD:]).astype(jnp.bfloat16)
                o_buf[pl.ds(i * width, width)] = o.reshape(width, count, HD)
                for j in range(width):
                    off = i * width + j

                    @pl.when(off > 0)
                    def _():
                        give_back(off).start()

    att[rank] = o_buf[0]

    @pl.loop(1, heads)
    def _(off):
        returned(off).wait_recv()

    feats = [att[h].astype(jnp.float32) for h in range(heads)]
    mean = jnp.sum(sum(feats), axis=1, keepdims=True) / (heads * HD)
    devs = [x - mean for x in feats]
    var = jnp.sum(sum(d * d for d in devs), axis=1, keepdims=True) / (heads * HD)
    inv = 1.0 / jnp.sqrt(var + 1e-06)
    normed = jnp.concatenate(
        [
            devs[h] * inv * (1.0 + scale_ref[h : h + 1, :]) + shift_ref[h : h + 1, :]
            for h in range(heads)
        ],
        axis=1,
    )
    patches = (
        lax.dot_general(
            normed,
            fw_ref[...],
            (((1,), (1,)), ((), ())),
            precision=lax.Precision.HIGHEST,
            preferred_element_type=jnp.float32,
        )
        + fb_ref[...]
    )
    patches = jnp.concatenate([patches, patches], axis=1)
    col = lax.rem(lax.broadcasted_iota(jnp.int32, patches.shape, 0), PC)
    shifted = (
        jnp.where(col == 0, 0.0, pltpu.roll(patches, 1, 0)),
        patches,
        jnp.where(col == PC - 1, 0.0, pltpu.roll(patches, count - 1, 0)),
    )
    lines = count // PC
    for sh in range(3):
        grid = shifted[sh].reshape(lines, PC, 2 * 64)
        if own < CB:
            grid = jnp.concatenate([grid, jnp.zeros((lines, CB, 2 * 64), jnp.float32)], axis=1)
        for tp in range(ntile):
            out_patch[tp, sh] = (
                grid[:, own * tp : own * tp + CB].reshape(lines * CB, 2 * 64).astype(jnp.bfloat16)
            )

    def patch_copy(dist, step, incoming=False):
        tp = lax.rem(t + step, ntile)
        origin = lax.rem(t - step + ntile, ntile) if incoming else t
        return pltpu.make_async_remote_copy(
            src_ref=out_patch.at[tp],
            dst_ref=in_patch.at[needed - dist, origin],
            send_sem=patch_send.at[dist, step],
            recv_sem=patch_recv.at[dist, step],
            device_id=(lax.rem(s + dist, nseq), tp),
            device_id_type=MESH,
        )

    for dist in reversed(range(needed + 1)):

        @pl.when(s + dist < nseq)
        def _():
            @pl.loop(0 if dist else 1, ntile)
            def _(step):
                patch_copy(dist, step).start()

    in_patch[needed, t] = out_patch[t]
    for dist in range(needed + 1):

        @pl.when(s >= dist)
        def _():
            @pl.loop(0 if dist else 1, ntile)
            def _(step):
                patch_copy(dist, step, True).wait_recv()

            lat_ref[needed - dist] = in_patch[needed - dist]

        @pl.when(s < dist)
        def _():
            lat_ref[needed - dist] = jnp.zeros_like(lat_ref[needed - dist])

    @pl.loop(1, heads)
    def _(off):
        for kind in range(3):
            outgoing(kind, off).wait_send()
        give_back(off).wait_send()

    for part in range(GROUPS):
        for other in range(1, members):
            relay(1, part, other).wait_send()
            relay(2, part, other).wait_send()
    for dist in range(needed + 1):

        @pl.when(s + dist < nseq)
        def _():
            @pl.loop(0 if dist else 1, ntile)
            def _(step):
                patch_copy(dist, step).wait_send()


def prepare_weights(win_ref, wup_ref, wx, wph):
    wx[...] = jnp.zeros_like(wx)
    for a in range(2):
        for b in range(2):
            for kx in range(3):
                half = (b + kx - 1) % 2
                for kt in range(3):
                    for i in range(2):
                        for line in range(2):
                            ky = 2 * (i - 1 + a) + line - a + 1
                            if 0 <= ky <= 2:
                                to = kt * 128 + i * 64 + (line * 2 + half) * 16
                                at = ((kt * 3 + ky) * 3 + kx) * 16
                                wx[a, b, kx, to : to + 16, :] = win_ref[at : at + 16, :]
    taps = (((0,), (1, 2)), ((0, 1), (2,)))
    for a in range(2):
        for b in range(2):
            for ty in range(2):
                for tx in range(2):
                    parts = [
                        wup_ref[ky * 3 + kx].astype(jnp.float32)
                        for ky in taps[a][ty]
                        for kx in taps[b][tx]
                    ]
                    wph[a, b, ty * 2 + tx] = sum(parts[1:], parts[0]).astype(jnp.bfloat16)


def conv_kernel(
    dims,
    tile_ref,
    widths_ref,
    lat_ref,
    win_ref,
    bin_ref,
    wup_ref,
    bup_ref,
    out_ref,
    wx,
    wph,
    mixed,
    wide,
    hidden,
    coef,
    cut,
):
    ntile, frames, lines, own = dims
    t = tile_ref[0]
    prepare_weights(win_ref, wup_ref, wx, wph)

    col = lax.broadcasted_iota(jnp.int32, (CB, 128), 0) + own * t
    starts, spans = [], []
    begin = jnp.int32(0)
    for k in range(ntile):
        starts.append(begin - OV)
        spans.append(widths_ref[k] + 2 * OV)
        begin = begin + widths_ref[k]
    for b in range(2):
        for px in range(2):
            x = 4 * col + 2 * b + px
            ramps = []
            for k in range(ntile):
                u = x - 2 * starts[k]
                dist = jnp.minimum(u, 2 * spans[k] - 1 - u) + 1
                ramps.append(jnp.clip(dist, 0, 4 * OV).astype(jnp.float32))
            scale = 1.0 / sum(ramps)
            for tx in range(2):
                full = left = right = jnp.zeros((CB, 128), jnp.float32)
                for k in range(ntile):
                    j = 2 * col + b + tx - 1 + px - starts[k]
                    share = ramps[k] * scale
                    left = left + jnp.where(j == 0, share, 0.0)
                    right = right + jnp.where(j == spans[k] - 1, share, 0.0)
                    full = full + jnp.where((j > 0) & (j < spans[k] - 1), share, 0.0)
                for v, c in enumerate((full, left, right)):
                    coef[b, px, tx, v] = c

    rows = PR * CB
    cut[...] = jnp.zeros_like(cut)
    lane = lax.broadcasted_iota(jnp.int32, (rows, 128), 1)
    blocks = PR // lines
    pad = jnp.zeros((CB, 128), jnp.float32)

    for frame in range(frames):
        first = lat_ref.shape[0] * frames - frames - 2 + frame
        for sh in range(3):
            pieces = ([], [])
            for kt in range(3):
                slot, inner = divmod(first + kt, frames)
                x = jnp.concatenate(
                    [lat_ref[slot, inner * blocks + i, sh] for i in range(blocks)], axis=0
                ).astype(jnp.float32)
                above = jnp.concatenate([pad, x[:-CB]], axis=0)
                below = jnp.concatenate([x[CB:], pad], axis=0)
                pieces[0].append(jnp.where(lane < 64, above, x).astype(jnp.bfloat16))
                pieces[1].append(jnp.where(lane < 64, x, below).astype(jnp.bfloat16))
            for a in range(2):
                cut[a, sh] = jnp.concatenate(pieces[a], axis=1)

        for a in range(2):
            for b in range(2):
                for kx in range(3):
                    low = (b + kx - 1) // 2 + 1 - b
                    source = jnp.concatenate([cut[a, low], cut[a, low + 1]], axis=0)
                    hidden[kx] = jnp.dot(
                        source, wx[a, b, kx], preferred_element_type=jnp.float32
                    ).reshape(2, PR, CB, -1)

                @pl.loop(0, PR)
                def _(r):
                    left, middle, right = (hidden[kx, :, r] for kx in range(3))
                    middle = middle + bin_ref[...][None]
                    hidden[0, :, r] = jax.nn.silu(left + middle + right)
                    hidden[1, :, r] = jax.nn.silu(middle + right)
                    hidden[2, :, r] = jax.nn.silu(left + middle)

                for hi in range(2):
                    place = 2 * hi - b
                    for ob in range(2):
                        for px in range(2):
                            tx = place + 1 - ob - px
                            if tx not in (0, 1):
                                continue
                            for part in range(0, hidden.shape[-1], 128):
                                lanes = slice(part, part + 128)
                                value = hidden[0, hi, :, :, lanes] * coef[ob, px, tx, 0][None]
                                for v in (1, 2):
                                    value = (
                                        value
                                        + hidden[v, hi, :, :, lanes] * coef[ob, px, tx, v][None]
                                    )
                                gone = jnp.zeros((1,) + value.shape[1:], jnp.float32)
                                if a == 0:
                                    moved = jnp.concatenate([value[1:], gone], axis=0)
                                    spots = (1, 3)
                                else:
                                    moved = jnp.concatenate([gone, value[:-1]], axis=0)
                                    spots = (2, 0)
                                for spot, val in zip(spots, (value, moved)):
                                    mixed[ob, px, tx, spot, :, lanes] = val.reshape(
                                        rows, 128
                                    ).astype(jnp.bfloat16)

        for ya in range(2):
            for px in range(2):
                total = None
                for ty in range(2):
                    for tx in range(2):
                        source = jnp.concatenate(
                            [
                                mixed[b, px, tx, a + ty + ya]
                                for a in range(2)
                                for b in range(2)
                            ],
                            axis=0,
                        )
                        term = jnp.dot(
                            source, wph[ya, px, ty * 2 + tx], preferred_element_type=jnp.float32
                        )
                        total = term if total is None else total + term
                total = (total + bup_ref[...]).reshape(2, 2, PR, CB, -1)
                for a in range(2):
                    for b in range(2):
                        for half in range(2):
                            wide[
                                half, :, 2 * a + ya, pl.ds(2 * b + px, CB, stride=4), :
                            ] = total[a, b, :, :, half * 128 : (half + 1) * 128]
        for half in range(2):
            out_ref[frame, :, :, half * 128 : (half + 1) * 128] = (
                wide[half, :, :, 0 : 4 * own, :]
                .reshape(4 * PR, 4 * own, -1)
                .astype(jnp.bfloat16)
            )


def per_device(
    queries,
    keys,
    values,
    mod_shift,
    mod_scale,
    final_weight,
    final_bias,
    tile_widths,
    conv_in_weight,
    conv_in_bias,
    conv_up_weight,
    conv_up_bias,
):
    nseq, ntile = lax.axis_size("seq"), lax.axis_size("tile")
    count, feat = queries.shape
    heads = feat // HD
    ndev = nseq * ntile
    members = ndev // heads
    lines = count // PC
    frames = count * ntile // (PR * PC)
    needed = -(-2 // frames)
    own = PC // ntile
    vmem = pl.BlockSpec(memory_space=pltpu.VMEM)
    lat_shape = (needed + 1, ntile, 3, lines * CB, 128)
    lat = pl.pallas_call(
        functools.partial(attention_kernel, (heads, nseq, ntile, needed, own)),
        out_shape=jax.ShapeDtypeStruct(lat_shape, jnp.bfloat16),
        in_specs=[vmem] * 7,
        out_specs=vmem,
        scratch_shapes=[
            pltpu.VMEM((heads, count, HD), jnp.bfloat16),
            pltpu.VMEM((members, heads, count, HD), jnp.bfloat16),
            pltpu.VMEM((members, heads, count, 2 * HD), jnp.bfloat16),
            pltpu.VMEM((heads * count, HD), jnp.float32),
            pltpu.VMEM((heads * count, 2 * HD), jnp.float32),
            pltpu.VMEM((heads, count, HD), jnp.bfloat16),
            pltpu.VMEM((heads, count, HD), jnp.bfloat16),
            pltpu.VMEM(lat_shape[1:], jnp.bfloat16),
            pltpu.VMEM(lat_shape, jnp.bfloat16),
            pltpu.SemaphoreType.DMA((3,)),
            pltpu.SemaphoreType.DMA((4, heads)),
            pltpu.SemaphoreType.DMA((4, heads)),
            pltpu.SemaphoreType.DMA((2, GROUPS, members)),
            pltpu.SemaphoreType.DMA((2, GROUPS, members)),
            pltpu.SemaphoreType.DMA((needed + 1, ntile)),
            pltpu.SemaphoreType.DMA((needed + 1, ntile)),
        ],
        compiler_params=pltpu.CompilerParams(
            collective_id=0, has_side_effects=True, vmem_limit_bytes=VMEM_LIMIT
        ),
    )(
        queries,
        keys,
        values,
        mod_shift.reshape(heads, HD),
        mod_scale.reshape(heads, HD),
        final_weight.T,
        final_bias.reshape(1, -1),
    )
    ch_in, ch_out = conv_up_weight.shape[1:]
    return pl.pallas_call(
        functools.partial(conv_kernel, (ntile, frames, lines, own)),
        out_shape=jax.ShapeDtypeStruct((frames, 4 * PR, 4 * own, ch_out), jnp.bfloat16),
        in_specs=[pl.BlockSpec(memory_space=pltpu.SMEM)] * 2 + [vmem] * 5,
        out_specs=vmem,
        scratch_shapes=[
            pltpu.VMEM((2, 2, 3, 384, ch_in), jnp.bfloat16),
            pltpu.VMEM((2, 2, 4, ch_in, ch_out), jnp.bfloat16),
            pltpu.VMEM((2, 2, 2, 4, PR * CB, ch_in), jnp.bfloat16),
            pltpu.VMEM((2, PR, 4, 4 * CB, 128), jnp.float32),
            pltpu.VMEM((3, 2, PR, CB, ch_in), jnp.float32),
            pltpu.VMEM((2, 2, 2, 3, CB, 128), jnp.float32),
            pltpu.VMEM((2, 3, PR * CB, 384), jnp.bfloat16),
        ],
        compiler_params=pltpu.CompilerParams(vmem_limit_bytes=VMEM_LIMIT),
    )(
        lax.axis_index("tile").reshape(1),
        tile_widths,
        lat,
        conv_in_weight,
        conv_in_bias.reshape(1, -1),
        conv_up_weight,
        conv_up_bias.reshape(1, -1),
    )


def solution(mesh):
    return jax.shard_map(
        per_device,
        mesh=mesh,
        in_specs=(P(("seq", "tile"), None),) * 3 + (P(),) * 9,
        out_specs=P("seq", None, "tile", None),
        check_vma=False,
    )
```
